32 devices in a mesh: groups: 2 (over x), gx: 16 (over z, y, core).
Axes of the slice: x: 2, y: 2, z: 4, core: 2. Of those that a mesh axis runs over, the one named last changes fastest.
Arguments:
- snapshots: float32 [256, 192, 8, 128], P('groups', 'gx'), parts along dimension 0, may hold values from -120 to 120
- coefficient: float32 [384, 8, 128], P(('groups', 'gx')), parts along dimension 0, may hold values from 0.5 to 4
Outputs:
- factor: float32 [256, 128], P('groups'), parts along dimension 0
- image: float32 [128, 384, 8, 128], P(None, ('groups', 'gx')), parts along dimension 1
- reduced: float32 [256, 128], P('groups'), parts along dimension 0
The draws below stay inside these ranges and needn't reach their ends.
There are 2 independent parts, one for each index of `groups`. The reference program is written for one: setup_inputs(seed, part) draws one part's arguments, and reference() takes and returns one part's arrays. A program takes and returns all parts, laid end to end along the dimension named above; each array names one. Nothing has to cross between parts.
All inputs are finite; a program needn't handle non-finite values.
Results may differ from the reference program's by a relative error of at most 0.00012.
Values sent between devices are 32-bit elements; how exact they have to be, the bound alone decides.
A program may use at most 128 MiB of HBM per device.

```python
import jax
import jax.numpy as jnp
from jax import lax

K = 128
CY = 8
CZ = 128
NX = 192


def draw_snapshots(key, part):
    keys = jax.random.split(jax.random.fold_in(key, 11), 4)
    scales = jnp.exp(jax.random.uniform(keys[0], (K, 1, 1, 1), jnp.float32, 0.0, 2.3))
    shares = jax.random.uniform(keys[1], (K, 1, 1, 1), jnp.float32, 0.2, 0.8)
    common = jnp.clip(jax.random.normal(keys[2], (1, NX, CY, CZ), jnp.float32), -6.0, 6.0)
    own = jnp.clip(jax.random.normal(keys[3], (K, NX, CY, CZ), jnp.float32), -6.0, 6.0)
    return scales * (shares * common + own)


def levels(rng, dims, shards, low, largest):
    gain, own = 1.0, jax.random.fold_in(rng, 6)
    for dim, shards_of in shards:
        draws = jnp.exp(jax.random.uniform(jax.random.fold_in(own, dim), (shards_of,), jnp.float32, low / len(shards), largest / len(shards)))
        gain = gain * jnp.repeat(draws, dims[dim] // shards_of).reshape([-1 if axis == dim else 1 for axis in range(len(dims))])
    return gain


def setup_inputs(seed: int = 0, part: int = 0) -> dict:
    arg_keys = jax.random.split(jax.random.key(seed), 3)
    own_keys = jax.random.split(jax.random.fold_in(arg_keys[2], part), 3)
    snapshots = draw_snapshots(jax.random.fold_in(jax.random.fold_in(arg_keys[2], part), 71), part)
    coefficient = jnp.clip(0.5 + 3.5 * jax.random.uniform(own_keys[1], (NX, CY, CZ), jnp.float32) ** levels(own_keys[1], (NX, CY, CZ), ((0, 16),), -0.2, 0.2), 0.5, 4.0)
    return dict(snapshots=snapshots, coefficient=coefficient)


HIGH = lax.Precision.HIGHEST

def apply_one(field, coefficient):
    padded = jnp.pad(field, 1)
    nx, ny, nz = field.shape
    total = jnp.zeros(field.shape, jnp.float32)
    for dx in range(3):
        for dy in range(3):
            for dz in range(3):
                if dx == 1 and dy == 1 and (dz == 1):
                    continue
                weight = 0.5 ** (abs(dx - 1) + abs(dy - 1) + abs(dz - 1))
                total = total + weight * padded[dx:dx + nx, dy:dy + ny, dz:dz + nz]
    return (8.0 + coefficient) * field - total

def reference(snapshots, coefficient):
    kdim = snapshots.shape[0]
    flat = snapshots.reshape(kdim, -1)
    ncells = flat.shape[1]
    gram = jnp.dot(flat.astype(jnp.float32), flat.T.astype(jnp.float32), precision=HIGH, preferred_element_type=jnp.float32) / ncells
    factor = jnp.linalg.cholesky(gram).T
    basis = jax.scipy.linalg.solve_triangular(factor.T, flat, lower=True)
    cube = basis.reshape(snapshots.shape)
    image = lax.map(lambda field: apply_one(field, coefficient), cube)
    reduced = jnp.dot(basis.astype(jnp.float32), image.reshape(kdim, -1).T.astype(jnp.float32), precision=HIGH, preferred_element_type=jnp.float32) / ncells
    return (factor, image, reduced)
```

```python
import functools

import jax
import jax.numpy as jnp
from jax import lax
from jax.experimental import pallas as pl
from jax.experimental.pallas import tpu as pltpu
from jax.sharding import PartitionSpec as P

MESH = pl.DeviceIdType.MESH
HIGH = lax.Precision.HIGHEST
F32, BF16 = jnp.float32, jnp.bfloat16
NT = (((1,), (1,)), ((), ()))
VMEM_BYTES = 48 * 2**20


def parts_of(value):
    high = value.astype(BF16)
    return high, (value - high.astype(F32)).astype(BF16)


def sweep(low, high, body, short):
    if short:
        for i in range(low, high):
            body(i)
    else:
        lax.fori_loop(low, high, lambda i, c: (body(i), c)[1], 0)


class Sum:
    def __init__(self, n, owners, terms, slots, total, sems):
        self.n, self.owners, self.every = n, owners, n // owners
        self.terms, self.slots, self.total = terms, slots, total
        self.send1, self.recv1, self.send2, self.recv2 = sems
        self.me = lax.axis_index("gx")
        self.own = self.me // self.every
        self.short = n <= 16

    def if_owner(self, device, body):
        if self.every == 1:
            body()
        else:
            pl.when(lax.rem(device, self.every) == 0)(body)

    def first(self, d):
        dest = lax.rem(self.me + d, self.n)
        return dest, pltpu.make_async_remote_copy(
            src_ref=self.terms.at[dest // self.every],
            dst_ref=self.slots.at[d],
            send_sem=self.send1.at[d],
            recv_sem=self.recv1.at[d],
            device_id={"gx": dest},
            device_id_type=MESH,
        )

    def second(self, d):
        dest = lax.rem(self.me + d, self.n)
        return pltpu.make_async_remote_copy(
            src_ref=self.total.at[self.own],
            dst_ref=self.total.at[self.own],
            send_sem=self.send2.at[d],
            recv_sem=self.recv2.at[self.own],
            device_id={"gx": dest},
            device_id_type=MESH,
        )

    def scatter(self):
        def go(d):
            dest, copy = self.first(d)
            self.if_owner(dest, copy.start)

        sweep(1, self.n, go, self.short)

    def spread(self):
        def add():
            sweep(1, self.n, lambda d: self.first(d)[1].wait_recv(), self.short)
            value = self.terms[self.own]
            if self.short:
                for d in range(1, self.n):
                    value = value + self.slots[d]
            else:
                value = lax.fori_loop(1, self.n, lambda d, v: v + self.slots[d], value)
            self.total[self.own] = value
            sweep(1, self.n, lambda d: self.second(d).start(), self.short)

        self.if_owner(self.me, add)

    def finish(self):
        def arrived(d):
            owner = lax.rem(self.own + d, self.owners)

            def wait():
                pltpu.make_async_remote_copy(
                    src_ref=self.total.at[owner],
                    dst_ref=self.total.at[owner],
                    send_sem=self.send2.at[0],
                    recv_sem=self.recv2.at[owner],
                    device_id={"gx": lax.rem(self.me + 1, self.n)},
                    device_id_type=MESH,
                ).wait_recv()

            if self.every == 1 and d == 0:
                return
            if d == 0:
                pl.when(lax.rem(self.me, self.every) != 0)(wait)
            else:
                wait()

        for d in range(self.owners):
            arrived(d)

        def sent(d):
            dest, copy = self.first(d)
            self.if_owner(dest, copy.wait_send)

        sweep(1, self.n, sent, self.short)
        self.if_owner(
            self.me, lambda: sweep(1, self.n, lambda d: self.second(d).wait_send(), self.short)
        )


def eliminate(rest, panels, start):
    done = []
    for panel in range(start, start + panels):
        rows, width = rest.shape
        lane = lax.broadcasted_iota(jnp.int32, (1, width), 1)
        row = lax.broadcasted_iota(jnp.int32, (rows, 1), 0)
        for j in range(8):
            at = panel * 8 + j
            here = lane == at
            column = rest[:, at : at + 1]
            pivot_row = rest[j : j + 1, :]
            scaled = jnp.where(here, 1.0, pivot_row) * (1.0 / column[j : j + 1, :])
            below = row > j
            column = jnp.where(below, column, 0.0)
            rest = jnp.where(jnp.logical_and(here, below), 0.0, rest) - column * scaled
        done.append(rest[:8])
        rest = rest[8:]
    return done, rest


def reduce_kernel(
    n, owners, snap, coef, packed, hsum, applied,
    s2, sb, ab, gt, gs, gtot, ht, hs, htot,
    load_sem, halo_send, halo_recv, out_sem,
    g0, g1, g2, g3, h0, h1, h2, h3,
):
    me = lax.axis_index("gx")
    cx, cy = s2.shape[0] - 2, s2.shape[1]
    kdim, cz = s2.shape[2], s2.shape[3]
    gram = Sum(n, owners, gt, gs, gtot, (g0, g1, g2, g3))
    hess = Sum(n, owners, ht, hs, htot, (h0, h1, h2, h3))

    barrier = pltpu.get_barrier_semaphore()

    def greet(d):
        pl.semaphore_signal(
            barrier, inc=1, device_id={"gx": lax.rem(me + d, n)}, device_id_type=MESH
        )

    sweep(1, n, greet, n <= 16)

    def load(x, y):
        return pltpu.make_async_copy(
            snap.at[:, x * cy + y, 0, :], s2.at[x + 1, y], load_sem.at[x, y]
        )

    def load_plane(i, c):
        for y in range(cy):
            load(lax.rem(i + cx - 1, cx), y).start()
        return c

    lax.fori_loop(0, cx, load_plane, 0)
    pl.semaphore_wait(barrier, n - 1)

    to_right = pltpu.make_async_remote_copy(
        src_ref=s2.at[cx], dst_ref=s2.at[0], send_sem=halo_send.at[0], recv_sem=halo_recv.at[0],
        device_id={"gx": lax.rem(me + 1, n)}, device_id_type=MESH,
    )
    to_left = pltpu.make_async_remote_copy(
        src_ref=s2.at[1], dst_ref=s2.at[cx + 1], send_sem=halo_send.at[1], recv_sem=halo_recv.at[1],
        device_id={"gx": lax.rem(me + n - 1, n)}, device_id_type=MESH,
    )

    def gram_plane(x):
        for y in range(cy):
            load(x, y).wait()
        if isinstance(x, int) and x == cx - 1:
            pl.when(me < n - 1)(to_right.start)
        if isinstance(x, int) and x == 0:
            pl.when(me > 0)(to_left.start)
        for y in range(cy):
            high, low = parts_of(s2[x + 1, y])
            sb[x, 0:kdim, y * cz : (y + 1) * cz] = high
            sb[x, kdim : 2 * kdim, y * cz : (y + 1) * cz] = low
        return lax.dot_general(sb[x], sb[x, 0:kdim], NT, preferred_element_type=F32)

    total = gram_plane(cx - 1) + gram_plane(0)
    total = lax.fori_loop(1, cx - 1, lambda x, t: t + gram_plane(x), total)
    cross = total[kdim:]
    gt[...] = (total[:kdim] + (cross + cross.T)).reshape(gt.shape)
    gram.scatter()

    lane = lax.broadcasted_iota(jnp.int32, (1, 1, cz), 2)
    from_low = jnp.where(lane == 0, 0.0, 0.5)
    from_high = jnp.where(lane == cz - 1, 0.0, 0.5)
    step = 16

    def stencil_plane(x):
        diag = 9.0 + coef[x]

        def rows(b, c):
            ks = pl.ds(pl.multiple_of(b * step, step), step)
            middle = s2[x + 1, :, ks, :]
            g = middle + 0.5 * (s2[x, :, ks, :] + s2[x + 2, :, ks, :])
            for y in range(cy):
                v = g[y]
                if y == 0:
                    v = v + 0.5 * g[1]
                elif y == cy - 1:
                    v = v + 0.5 * g[cy - 2]
                else:
                    v = v + 0.5 * (g[y - 1] + g[y + 1])
                v = (
                    v
                    + from_low[0] * pltpu.roll(v, 1, 1)
                    + from_high[0] * pltpu.roll(v, cz - 1, 1)
                )
                high, low = parts_of(diag[y : y + 1, :] * middle[y] - v)
                ab[x, ks, y * cz : (y + 1) * cz] = high
                ab[x, pl.ds(pl.multiple_of(kdim + b * step, step), step), y * cz : (y + 1) * cz] = low
            return c

        lax.fori_loop(0, kdim // step, rows, 0)
        pltpu.make_async_copy(ab.at[x], applied.at[x], out_sem.at[x]).start()
        return lax.dot_general(
            sb[x], ab[x, 0:kdim], NT, preferred_element_type=F32
        ), lax.dot_general(sb[x, 0:kdim], ab[x, kdim : 2 * kdim], NT, preferred_element_type=F32)

    def stencil_sum(x, t):
        a, b = stencil_plane(x)
        return t[0] + a, t[1] + b

    zero = (jnp.zeros((2 * kdim, kdim), F32), jnp.zeros((kdim, kdim), F32))
    half = cx // 2
    t = lax.fori_loop(1, half, stencil_sum, zero)
    gram.spread()
    t = lax.fori_loop(half, cx - 1, stencil_sum, t)

    @pl.when(me > 0)
    def _():
        to_right.wait_recv()

    @pl.when(me == 0)
    def _():
        s2[0] = jnp.zeros(s2.shape[1:], F32)

    t = stencil_sum(0, t)

    @pl.when(me < n - 1)
    def _():
        to_left.wait_recv()

    @pl.when(me == n - 1)
    def _():
        s2[cx + 1] = jnp.zeros(s2.shape[1:], F32)

    t = stencil_sum(cx - 1, t)
    ht[...] = (t[0][:kdim] + t[0][kdim:] + t[1]).reshape(ht.shape)
    hess.scatter()

    gram.finish()
    ncells = cx * n * cy * cz
    rest = gtot[...].reshape(kdim, kdim) * (1.0 / ncells)
    panels = kdim // 8
    done, rest = eliminate(rest, panels // 2, 0)
    hess.spread()
    more, rest = eliminate(rest, panels - panels // 2, panels // 2)
    packed[...] = jnp.concatenate(done + more, axis=0)
    hess.finish()
    hsum[...] = htot[...].reshape(kdim, kdim) * (1.0 / ncells)

    pl.when(me < n - 1)(to_right.wait_send)
    pl.when(me > 0)(to_left.wait_send)

    def written(x, c):
        pltpu.make_async_copy(ab.at[x], applied.at[x], out_sem.at[x]).wait()
        return c

    lax.fori_loop(0, cx, written, 0)


def image_kernel(packed, hsum, applied, factor, image, reduced, ab, buf, load_sem, out_sem):
    cx, cy, kdim, cz = buf.shape

    def load(x):
        return pltpu.make_async_copy(applied.at[x], ab.at[x], load_sem.at[x])

    def start(x, c):
        load(x).start()
        return c

    lax.fori_loop(0, cx, start, 0)
    a = packed[...]
    row = lax.broadcasted_iota(jnp.int32, (kdim, kdim), 0)
    col = lax.broadcasted_iota(jnp.int32, (kdim, kdim), 1)
    pivots = jnp.sum(jnp.where(row == col, a, 0.0), axis=1, keepdims=True)
    scale = 1.0 / jnp.sqrt(pivots)
    factor[...] = jnp.where(col >= row, a * scale, 0.0)
    inverse = jnp.where(col < row, a, jnp.where(row == col, 1.0, 0.0)) * scale
    high, low = parts_of(inverse)
    twice = jnp.concatenate([high, high], axis=1)

    def store(x, y):
        return pltpu.make_async_copy(
            buf.at[x, y], image.at[:, x * cy + y, 0, :], out_sem.at[x, y]
        )

    def plane(x, c):
        load(x).wait()
        for y in range(0, cy, 2):
            at = slice(y * cz, (y + 2) * cz)
            value = jnp.dot(twice, ab[x, :, at], preferred_element_type=F32) + jnp.dot(
                low, ab[x, 0:kdim, at], preferred_element_type=F32
            )
            buf[x, y] = value[:, :cz]
            buf[x, y + 1] = value[:, cz:]
            store(x, y).start()
            store(x, y + 1).start()
        return c

    lax.fori_loop(0, cx, plane, 0)
    left = jnp.dot(inverse, hsum[...], precision=HIGH, preferred_element_type=F32)
    reduced[...] = lax.dot_general(left, inverse, NT, precision=HIGH, preferred_element_type=F32)

    def finish(x, c):
        for y in range(cy):
            store(x, y).wait()
        return c

    lax.fori_loop(0, cx, finish, 0)


def shards(n, snapshots, coefficient):
    kdim, cx, cy, cz = snapshots.shape
    owners = min(n, kdim // 8)
    rows = kdim // owners
    vmem = pl.BlockSpec(memory_space=pltpu.VMEM)
    hbm = pl.BlockSpec(memory_space=pl.ANY)
    square = jax.ShapeDtypeStruct((kdim, kdim), F32)
    dma = pltpu.SemaphoreType.DMA
    summed = [
        pltpu.VMEM((owners, rows, kdim), F32),
        pltpu.VMEM((n, rows, kdim), F32),
        pltpu.VMEM((owners, rows, kdim), F32),
    ]
    sum_sems = [dma((n,)), dma((n,)), dma((n,)), dma((owners,))]
    packed, hsum, applied = pl.pallas_call(
        functools.partial(reduce_kernel, n, owners),
        out_shape=(square, square, jax.ShapeDtypeStruct((cx, 2 * kdim, cy * cz), BF16)),
        in_specs=[hbm, vmem],
        out_specs=(vmem, vmem, hbm),
        scratch_shapes=[
            pltpu.VMEM((cx + 2, cy, kdim, cz), F32),
            pltpu.VMEM((cx, 2 * kdim, cy * cz), BF16),
            pltpu.VMEM((cx, 2 * kdim, cy * cz), BF16),
            *summed,
            *summed,
            dma((cx, cy)), dma((2,)), dma((2,)), dma((cx,)),
            *sum_sems,
            *sum_sems,
        ],
        compiler_params=pltpu.CompilerParams(
            collective_id=0, has_side_effects=True, vmem_limit_bytes=VMEM_BYTES
        ),
        name="reduce_kernel",
    )(snapshots.reshape(kdim, cx * cy, 1, cz), coefficient)
    factor, image, reduced = pl.pallas_call(
        image_kernel,
        out_shape=(square, jax.ShapeDtypeStruct((kdim, cx * cy, 1, cz), F32), square),
        in_specs=[vmem, vmem, hbm],
        out_specs=(vmem, hbm, vmem),
        scratch_shapes=[
            pltpu.VMEM((cx, 2 * kdim, cy * cz), BF16),
            pltpu.VMEM((cx, cy, kdim, cz), F32),
            dma((cx,)), dma((cx, cy)),
        ],
        compiler_params=pltpu.CompilerParams(vmem_limit_bytes=VMEM_BYTES),
        name="image_kernel",
    )(packed, hsum, applied)
    return factor, image.reshape(kdim, cx, cy, cz), reduced


def solution(mesh):
    placed = (P("groups", "gx", None, None), P(("groups", "gx"), None, None))
    return jax.shard_map(
        functools.partial(shards, mesh.shape["gx"]),
        mesh=mesh,
        in_specs=placed,
        out_specs=(P("groups", None), P(None, ("groups", "gx"), None, None), P("groups", None)),
        check_vma=False,
    )
```

```python
import functools

import jax
import jax.numpy as jnp
from jax import lax
from jax.experimental import pallas as pl
from jax.experimental.pallas import tpu as pltpu
from jax.sharding import PartitionSpec as P

MESH = pl.DeviceIdType.MESH
HIGH = lax.Precision.HIGHEST
F32, BF16 = jnp.float32, jnp.bfloat16
NT = (((1,), (1,)), ((), ()))
VMEM_BYTES = 48 * 2**20


def parts_of(value):
    high = value.astype(BF16)
    return high, (value - high.astype(F32)).astype(BF16)


def sweep(low, high, body, short):
    if short:
        for i in range(low, high):
            body(i)
    else:
        lax.fori_loop(low, high, lambda i, c: (body(i), c)[1], 0)


class Sum:
    def __init__(self, n, owners, terms, slots, total, sems):
        self.n, self.owners, self.every = n, owners, n // owners
        self.terms, self.slots, self.total = terms, slots, total
        self.send1, self.recv1, self.send2, self.recv2 = sems
        self.me = lax.axis_index("gx")
        self.own = self.me // self.every
        self.short = n <= 16

    def if_owner(self, device, body):
        if self.every == 1:
            body()
        else:
            pl.when(lax.rem(device, self.every) == 0)(body)

    def first(self, d):
        dest = lax.rem(self.me + d, self.n)
        return dest, pltpu.make_async_remote_copy(
            src_ref=self.terms.at[dest // self.every],
            dst_ref=self.slots.at[d],
            send_sem=self.send1.at[d],
            recv_sem=self.recv1.at[d],
            device_id={"gx": dest},
            device_id_type=MESH,
        )

    def second(self, d):
        dest = lax.rem(self.me + d, self.n)
        return pltpu.make_async_remote_copy(
            src_ref=self.total.at[self.own],
            dst_ref=self.total.at[self.own],
            send_sem=self.send2.at[d],
            recv_sem=self.recv2.at[self.own],
            device_id={"gx": dest},
            device_id_type=MESH,
        )

    def scatter(self):
        def go(d):
            dest, copy = self.first(d)
            self.if_owner(dest, copy.start)

        sweep(1, self.n, go, self.short)

    def spread(self):
        def add():
            sweep(1, self.n, lambda d: self.first(d)[1].wait_recv(), self.short)
            value = self.terms[self.own]
            if self.short:
                for d in range(1, self.n):
                    value = value + self.slots[d]
            else:
                value = lax.fori_loop(1, self.n, lambda d, v: v + self.slots[d], value)
            self.total[self.own] = value
            sweep(1, self.n, lambda d: self.second(d).start(), self.short)

        self.if_owner(self.me, add)

    def finish(self):
        def arrived(d):
            owner = lax.rem(self.own + d, self.owners)

            def wait():
                pltpu.make_async_remote_copy(
                    src_ref=self.total.at[owner],
                    dst_ref=self.total.at[owner],
                    send_sem=self.send2.at[0],
                    recv_sem=self.recv2.at[owner],
                    device_id={"gx": lax.rem(self.me + 1, self.n)},
                    device_id_type=MESH,
                ).wait_recv()

            if self.every == 1 and d == 0:
                return
            if d == 0:
                pl.when(lax.rem(self.me, self.every) != 0)(wait)
            else:
                wait()

        for d in range(self.owners):
            arrived(d)

        def sent(d):
            dest, copy = self.first(d)
            self.if_owner(dest, copy.wait_send)

        sweep(1, self.n, sent, self.short)
        self.if_owner(
            self.me, lambda: sweep(1, self.n, lambda d: self.second(d).wait_send(), self.short)
        )


def eliminate(rest, panels, start):
    done = []
    width = rest.shape[1]
    lane = lax.broadcasted_iota(jnp.int32, (1, width), 1)
    row = lax.broadcasted_iota(jnp.int32, (8, 1), 0)
    for panel in range(start, start + panels):
        head, tail = rest[:8], rest[8:]
        for j in range(0, 8, 2):
            at = panel * 8 + j
            one, two = lane == at, lane == at + 1
            either = jnp.logical_or(one, two)
            first, second = head[j : j + 1], head[j + 1 : j + 2]
            c1, c2 = head[:, at : at + 1], head[:, at + 1 : at + 2]
            p11, p12, p22 = c1[j : j + 1], c2[j : j + 1], c2[j + 1 : j + 2]
            inverse = 1.0 / (p11 * p22 - p12 * p12)
            row1 = jnp.where(one, 1.0, jnp.where(two, 0.0, first))
            row2 = jnp.where(two, 1.0, jnp.where(one, 0.0, second))
            q1 = (p22 * row1 - p12 * row2) * inverse
            q2 = (p11 * row2 - p12 * row1) * inverse
            if panel * 8 + 8 < width:
                t1, t2 = tail[:, at : at + 1], tail[:, at + 1 : at + 2]
                tail = jnp.where(either, 0.0, tail) - (t1 * q1 + t2 * q2)
            pair = jnp.where(one, 0.0, second) - (p12 / p11) * jnp.where(one, 1.0, first)
            lower = jnp.where(either, 0.0, head) - (c1 * q1 + c2 * q2)
            head = jnp.where(row > j + 1, lower, jnp.where(row == j + 1, pair, head))
        done.append(head)
        rest = tail
    return done, rest


def reduce_kernel(
    n, owners, snap, coef, packed, hsum, applied,
    s2, sb, ab, hacc, hlow, gt, gs, gtot, ht, hs, htot,
    load_sem, halo_send, halo_recv, out_sem,
    g0, g1, g2, g3, h0, h1, h2, h3,
):
    me = lax.axis_index("gx")
    cx, cy = s2.shape[0] - 2, s2.shape[1]
    kdim, cz = s2.shape[2], s2.shape[3]
    gram = Sum(n, owners, gt, gs, gtot, (g0, g1, g2, g3))
    hess = Sum(n, owners, ht, hs, htot, (h0, h1, h2, h3))

    barrier = pltpu.get_barrier_semaphore()

    def greet(d):
        pl.semaphore_signal(
            barrier, inc=1, device_id={"gx": lax.rem(me + d, n)}, device_id_type=MESH
        )

    sweep(1, n, greet, n <= 16)

    def load(x, y):
        return pltpu.make_async_copy(
            snap.at[:, x * cy + y, 0, :], s2.at[x + 1, y], load_sem.at[x, y]
        )

    def load_plane(i, c):
        for y in range(cy):
            load(lax.rem(i + cx - 1, cx), y).start()
        return c

    lax.fori_loop(0, cx, load_plane, 0)
    pl.semaphore_wait(barrier, n - 1)

    to_right = pltpu.make_async_remote_copy(
        src_ref=s2.at[cx], dst_ref=s2.at[0], send_sem=halo_send.at[0], recv_sem=halo_recv.at[0],
        device_id={"gx": lax.rem(me + 1, n)}, device_id_type=MESH,
    )
    to_left = pltpu.make_async_remote_copy(
        src_ref=s2.at[1], dst_ref=s2.at[cx + 1], send_sem=halo_send.at[1], recv_sem=halo_recv.at[1],
        device_id={"gx": lax.rem(me + n - 1, n)}, device_id_type=MESH,
    )

    def gram_plane(x):
        for y in range(cy):
            load(x, y).wait()
        if isinstance(x, int) and x == cx - 1:
            pl.when(me < n - 1)(to_right.start)
        if isinstance(x, int) and x == 0:
            pl.when(me > 0)(to_left.start)
        for y in range(cy):
            high, low = parts_of(s2[x + 1, y])
            sb[x, 0:kdim, y * cz : (y + 1) * cz] = high
            sb[x, kdim : 2 * kdim, y * cz : (y + 1) * cz] = low
        return lax.dot_general(sb[x], sb[x, 0:kdim], NT, preferred_element_type=F32)

    total = gram_plane(cx - 1) + gram_plane(0)
    total = lax.fori_loop(1, cx - 1, lambda x, t: t + gram_plane(x), total)
    cross = total[kdim:]
    gt[...] = (total[:kdim] + (cross + cross.T)).reshape(gt.shape)
    gram.scatter()

    lane = lax.broadcasted_iota(jnp.int32, (1, 1, cz), 2)
    from_low = jnp.where(lane == 0, 0.0, 0.5)
    from_high = jnp.where(lane == cz - 1, 0.0, 0.5)
    step = 16
    groups = kdim // step // (cy // 2)

    def stencil_plane(x, before):
        diag = 9.0 + coef[x]

        def chunk(b, c):
            if before is not None:
                products(before, b)
            for part in range(groups):
                rows(b * groups + part)
            return c

        def rows(b):
            ks = pl.ds(pl.multiple_of(b * step, step), step)
            middle = s2[x + 1, :, ks, :]
            g = middle + 0.5 * (s2[x, :, ks, :] + s2[x + 2, :, ks, :])
            for y in range(cy):
                v = g[y]
                if y == 0:
                    v = v + 0.5 * g[1]
                elif y == cy - 1:
                    v = v + 0.5 * g[cy - 2]
                else:
                    v = v + 0.5 * (g[y - 1] + g[y + 1])
                v = (
                    v
                    + from_low[0] * pltpu.roll(v, 1, 1)
                    + from_high[0] * pltpu.roll(v, cz - 1, 1)
                )
                high, low = parts_of(diag[y : y + 1, :] * middle[y] - v)
                ab[x, ks, y * cz : (y + 1) * cz] = high
                ab[x, pl.ds(pl.multiple_of(kdim + b * step, step), step), y * cz : (y + 1) * cz] = low

        lax.fori_loop(0, cy // 2, chunk, 0)
        pltpu.make_async_copy(ab.at[x], applied.at[x], out_sem.at[x]).start()

    def products(x, b):
        at = pl.ds(pl.multiple_of(b * 2 * cz, 2 * cz), 2 * cz)
        hacc[...] += lax.dot_general(
            sb[x, :, at], ab[x, 0:kdim, at], NT, preferred_element_type=F32
        )
        hlow[...] += lax.dot_general(
            sb[x, 0:kdim, at], ab[x, kdim : 2 * kdim, at], NT, preferred_element_type=F32
        )

    def all_products(x):
        for b in range(cy // 2):
            products(x, b)

    def stencil_next(x, c):
        stencil_plane(x, x - 1)
        return c

    hacc[...] = jnp.zeros(hacc.shape, F32)
    hlow[...] = jnp.zeros(hlow.shape, F32)
    half = cx // 2
    stencil_plane(1, None)
    lax.fori_loop(2, half, stencil_next, 0)
    gram.spread()
    lax.fori_loop(half, cx - 1, stencil_next, 0)

    @pl.when(me > 0)
    def _():
        to_right.wait_recv()

    @pl.when(me == 0)
    def _():
        s2[0] = jnp.zeros(s2.shape[1:], F32)

    stencil_plane(0, cx - 2)

    @pl.when(me < n - 1)
    def _():
        to_left.wait_recv()

    @pl.when(me == n - 1)
    def _():
        s2[cx + 1] = jnp.zeros(s2.shape[1:], F32)

    stencil_plane(cx - 1, 0)
    all_products(cx - 1)
    ht[...] = (hacc[:kdim] + hacc[kdim:] + hlow[...]).reshape(ht.shape)
    hess.scatter()

    gram.finish()
    ncells = cx * n * cy * cz
    full = gtot[...].reshape(kdim, kdim) * (1.0 / ncells)
    rows, cols = (lax.broadcasted_iota(jnp.int32, (kdim, kdim), d) for d in (0, 1))
    on_diagonal = jnp.where(rows == cols, full, 0.0)
    norm = jnp.sqrt(jnp.sum(on_diagonal, axis=0, keepdims=True))
    inv_norm = 1.0 / norm
    rest = full * inv_norm * (1.0 / jnp.sqrt(jnp.sum(on_diagonal, axis=1, keepdims=True)))
    panels = kdim // 8
    done, rest = eliminate(rest, panels // 2, 0)
    hess.spread()
    more, rest = eliminate(rest, panels - panels // 2, panels // 2)
    rest = jnp.concatenate(done + more, axis=0)
    pivots = jnp.sum(jnp.where(rows == cols, rest, 0.0), axis=1, keepdims=True)
    packed[...] = rest * (1.0 / jnp.sqrt(pivots)) * jnp.where(cols >= rows, norm, inv_norm)
    hess.finish()
    hsum[...] = htot[...].reshape(kdim, kdim) * (1.0 / ncells)

    pl.when(me < n - 1)(to_right.wait_send)
    pl.when(me > 0)(to_left.wait_send)

    def written(x, c):
        pltpu.make_async_copy(ab.at[x], applied.at[x], out_sem.at[x]).wait()
        return c

    lax.fori_loop(0, cx, written, 0)


def image_kernel(packed, hsum, applied, factor, image, reduced, ab, buf, load_sem, out_sem):
    cx, cy, kdim, cz = buf.shape

    def load(x):
        return pltpu.make_async_copy(applied.at[x], ab.at[x], load_sem.at[x])

    def start(x, c):
        load(x).start()
        return c

    lax.fori_loop(0, cx, start, 0)
    a = packed[...]
    row = lax.broadcasted_iota(jnp.int32, (kdim, kdim), 0)
    col = lax.broadcasted_iota(jnp.int32, (kdim, kdim), 1)
    pivots = jnp.sum(jnp.where(row == col, a, 0.0), axis=1, keepdims=True)
    factor[...] = jnp.where(col >= row, a, 0.0)
    inverse = jnp.where(col < row, a, jnp.where(row == col, 1.0 / pivots, 0.0))
    high, low = parts_of(inverse)
    twice = jnp.concatenate([high, high], axis=1)

    def store(x, y):
        return pltpu.make_async_copy(
            buf.at[x, y], image.at[:, x * cy + y, 0, :], out_sem.at[x, y]
        )

    def plane(x, c):
        load(x).wait()
        for y in range(0, cy, 2):
            at = slice(y * cz, (y + 2) * cz)
            value = jnp.dot(twice, ab[x, :, at], preferred_element_type=F32) + jnp.dot(
                low, ab[x, 0:kdim, at], preferred_element_type=F32
            )
            buf[x, y] = value[:, :cz]
            buf[x, y + 1] = value[:, cz:]
            store(x, y).start()
            store(x, y + 1).start()
        return c

    lax.fori_loop(0, cx, plane, 0)
    left = jnp.dot(inverse, hsum[...], precision=HIGH, preferred_element_type=F32)
    reduced[...] = lax.dot_general(left, inverse, NT, precision=HIGH, preferred_element_type=F32)

    def finish(x, c):
        for y in range(cy):
            store(x, y).wait()
        return c

    lax.fori_loop(0, cx, finish, 0)


def shards(n, snapshots, coefficient):
    kdim, cx, cy, cz = snapshots.shape
    owners = min(n, kdim // 8)
    rows = kdim // owners
    vmem = pl.BlockSpec(memory_space=pltpu.VMEM)
    hbm = pl.BlockSpec(memory_space=pl.ANY)
    square = jax.ShapeDtypeStruct((kdim, kdim), F32)
    dma = pltpu.SemaphoreType.DMA
    summed = [
        pltpu.VMEM((owners, rows, kdim), F32),
        pltpu.VMEM((n, rows, kdim), F32),
        pltpu.VMEM((owners, rows, kdim), F32),
    ]
    sum_sems = [dma((n,)), dma((n,)), dma((n,)), dma((owners,))]
    packed, hsum, applied = pl.pallas_call(
        functools.partial(reduce_kernel, n, owners),
        out_shape=(square, square, jax.ShapeDtypeStruct((cx, 2 * kdim, cy * cz), BF16)),
        in_specs=[hbm, vmem],
        out_specs=(vmem, vmem, hbm),
        scratch_shapes=[
            pltpu.VMEM((cx + 2, cy, kdim, cz), F32),
            pltpu.VMEM((cx, 2 * kdim, cy * cz), BF16),
            pltpu.VMEM((cx, 2 * kdim, cy * cz), BF16),
            pltpu.VMEM((2 * kdim, kdim), F32),
            pltpu.VMEM((kdim, kdim), F32),
            *summed,
            *summed,
            dma((cx, cy)), dma((2,)), dma((2,)), dma((cx,)),
            *sum_sems,
            *sum_sems,
        ],
        compiler_params=pltpu.CompilerParams(
            collective_id=0, has_side_effects=True, vmem_limit_bytes=VMEM_BYTES
        ),
        name="reduce_kernel",
    )(snapshots.reshape(kdim, cx * cy, 1, cz), coefficient)
    factor, image, reduced = pl.pallas_call(
        image_kernel,
        out_shape=(square, jax.ShapeDtypeStruct((kdim, cx * cy, 1, cz), F32), square),
        in_specs=[vmem, vmem, hbm],
        out_specs=(vmem, hbm, vmem),
        scratch_shapes=[
            pltpu.VMEM((cx, 2 * kdim, cy * cz), BF16),
            pltpu.VMEM((cx, cy, kdim, cz), F32),
            dma((cx,)), dma((cx, cy)),
        ],
        compiler_params=pltpu.CompilerParams(vmem_limit_bytes=VMEM_BYTES),
        name="image_kernel",
    )(packed, hsum, applied)
    return factor, image.reshape(kdim, cx, cy, cz), reduced


def solution(mesh):
    placed = (P("groups", "gx", None, None), P(("groups", "gx"), None, None))
    return jax.shard_map(
        functools.partial(shards, mesh.shape["gx"]),
        mesh=mesh,
        in_specs=placed,
        out_specs=(P("groups", None), P(None, ("groups", "gx"), None, None), P("groups", None)),
        check_vma=False,
    )
```

```python
import functools

import jax
import jax.numpy as jnp
from jax import lax
from jax.experimental import pallas as pl
from jax.experimental.pallas import tpu as pltpu
from jax.sharding import PartitionSpec as P

MESH = pl.DeviceIdType.MESH
HIGH = lax.Precision.HIGHEST
F32, BF16 = jnp.float32, jnp.bfloat16
NT = (((1,), (1,)), ((), ()))
VMEM_BYTES = 48 * 2**20


def parts_of(value):
    high = value.astype(BF16)
    return high, (value - high.astype(F32)).astype(BF16)


def sweep(low, high, body, short):
    if short:
        for i in range(low, high):
            body(i)
    else:
        lax.fori_loop(low, high, lambda i, c: (body(i), c)[1], 0)


class Sum:
    def __init__(self, n, owners, terms, slots, total, sems):
        self.n, self.owners, self.every = n, owners, n // owners
        self.terms, self.slots, self.total = terms, slots, total
        self.send1, self.recv1, self.send2, self.recv2 = sems
        self.me = lax.axis_index("gx")
        self.own = self.me // self.every
        self.short = n <= 16

    def if_owner(self, device, body):
        if self.every == 1:
            body()
        else:
            pl.when(lax.rem(device, self.every) == 0)(body)

    def first(self, d):
        dest = lax.rem(self.me + d, self.n)
        return dest, pltpu.make_async_remote_copy(
            src_ref=self.terms.at[dest // self.every],
            dst_ref=self.slots.at[d],
            send_sem=self.send1.at[d],
            recv_sem=self.recv1.at[d],
            device_id={"gx": dest},
            device_id_type=MESH,
        )

    def second(self, d):
        dest = lax.rem(self.me + d, self.n)
        return pltpu.make_async_remote_copy(
            src_ref=self.total.at[self.own],
            dst_ref=self.total.at[self.own],
            send_sem=self.send2.at[d],
            recv_sem=self.recv2.at[self.own],
            device_id={"gx": dest},
            device_id_type=MESH,
        )

    def scatter(self):
        def go(d):
            dest, copy = self.first(d)
            self.if_owner(dest, copy.start)

        sweep(1, self.n, go, self.short)

    def spread(self):
        def add():
            sweep(1, self.n, lambda d: self.first(d)[1].wait_recv(), self.short)
            value = self.terms[self.own]
            if self.short:
                for d in range(1, self.n):
                    value = value + self.slots[d]
            else:
                value = lax.fori_loop(1, self.n, lambda d, v: v + self.slots[d], value)
            self.total[self.own] = value
            sweep(1, self.n, lambda d: self.second(d).start(), self.short)

        self.if_owner(self.me, add)

    def finish(self):
        def arrived(d):
            owner = lax.rem(self.own + d, self.owners)

            def wait():
                pltpu.make_async_remote_copy(
                    src_ref=self.total.at[owner],
                    dst_ref=self.total.at[owner],
                    send_sem=self.send2.at[0],
                    recv_sem=self.recv2.at[owner],
                    device_id={"gx": lax.rem(self.me + 1, self.n)},
                    device_id_type=MESH,
                ).wait_recv()

            if self.every == 1 and d == 0:
                return
            if d == 0:
                pl.when(lax.rem(self.me, self.every) != 0)(wait)
            else:
                wait()

        for d in range(self.owners):
            arrived(d)

        def sent(d):
            dest, copy = self.first(d)
            self.if_owner(dest, copy.wait_send)

        sweep(1, self.n, sent, self.short)
        self.if_owner(
            self.me, lambda: sweep(1, self.n, lambda d: self.second(d).wait_send(), self.short)
        )


def eliminate(rest, panels, start):
    done = []
    width = rest.shape[1]
    lane = lax.broadcasted_iota(jnp.int32, (1, width), 1)
    row = lax.broadcasted_iota(jnp.int32, (8, 1), 0)
    for panel in range(start, start + panels):
        head, tail = rest[:8], rest[8:]
        for j in range(0, 8, 2):
            at = panel * 8 + j
            one, two = lane == at, lane == at + 1
            either = jnp.logical_or(one, two)
            first, second = head[j : j + 1], head[j + 1 : j + 2]
            c1, c2 = head[:, at : at + 1], head[:, at + 1 : at + 2]
            p11, p12, p22 = c1[j : j + 1], c2[j : j + 1], c2[j + 1 : j + 2]
            inverse = 1.0 / (p11 * p22 - p12 * p12)
            row1 = jnp.where(one, 1.0, jnp.where(two, 0.0, first))
            row2 = jnp.where(two, 1.0, jnp.where(one, 0.0, second))
            q1 = (p22 * row1 - p12 * row2) * inverse
            q2 = (p11 * row2 - p12 * row1) * inverse
            if panel * 8 + 8 < width:
                t1, t2 = tail[:, at : at + 1], tail[:, at + 1 : at + 2]
                tail = jnp.where(either, 0.0, tail) - (t1 * q1 + t2 * q2)
            pair = jnp.where(one, 0.0, second) - (p12 / p11) * jnp.where(one, 1.0, first)
            lower = jnp.where(either, 0.0, head) - (c1 * q1 + c2 * q2)
            head = jnp.where(row > j + 1, lower, jnp.where(row == j + 1, pair, head))
        done.append(head)
        rest = tail
    return done, rest


def reduce_kernel(
    n, owners, snap, coef_in, packed, hsum, applied,
    coef, coef_sem, s2, sb, ab, hacc, hlow, gt, gs, gtot, ht, hs, htot,
    load_sem, halo_send, halo_recv, out_sem,
    g0, g1, g2, g3, h0, h1, h2, h3,
):
    me = lax.axis_index("gx")
    cx, cy = s2.shape[0] - 2, s2.shape[1]
    kdim, cz = s2.shape[2], s2.shape[3]
    gram = Sum(n, owners, gt, gs, gtot, (g0, g1, g2, g3))
    hess = Sum(n, owners, ht, hs, htot, (h0, h1, h2, h3))

    barrier = pltpu.get_barrier_semaphore()

    def greet(d):
        pl.semaphore_signal(
            barrier, inc=1, device_id={"gx": lax.rem(me + d, n)}, device_id_type=MESH
        )

    sweep(1, n, greet, n <= 16)

    def load(x, y):
        return pltpu.make_async_copy(
            snap.at[:, x * cy + y, 0, :], s2.at[x + 1, y], load_sem.at[x, y]
        )

    def load_plane(i, c):
        for y in range(cy):
            load(lax.rem(i + cx - 1, cx), y).start()
        return c

    lax.fori_loop(0, cx, load_plane, 0)
    coefficients = pltpu.make_async_copy(coef_in, coef, coef_sem)
    coefficients.start()
    pl.semaphore_wait(barrier, n - 1)

    to_right = pltpu.make_async_remote_copy(
        src_ref=s2.at[cx], dst_ref=s2.at[0], send_sem=halo_send.at[0], recv_sem=halo_recv.at[0],
        device_id={"gx": lax.rem(me + 1, n)}, device_id_type=MESH,
    )
    to_left = pltpu.make_async_remote_copy(
        src_ref=s2.at[1], dst_ref=s2.at[cx + 1], send_sem=halo_send.at[1], recv_sem=halo_recv.at[1],
        device_id={"gx": lax.rem(me + n - 1, n)}, device_id_type=MESH,
    )

    def gram_plane(x):
        for y in range(cy):
            load(x, y).wait()
        if isinstance(x, int) and x == cx - 1:
            pl.when(me < n - 1)(to_right.start)
        if isinstance(x, int) and x == 0:
            pl.when(me > 0)(to_left.start)
        for y in range(cy):
            high, low = parts_of(s2[x + 1, y])
            sb[x, 0:kdim, y * cz : (y + 1) * cz] = high
            sb[x, kdim : 2 * kdim, y * cz : (y + 1) * cz] = low
        return lax.dot_general(sb[x], sb[x, 0:kdim], NT, preferred_element_type=F32)

    total = gram_plane(cx - 1) + gram_plane(0)
    total = lax.fori_loop(1, cx - 1, lambda x, t: t + gram_plane(x), total, unroll=2)
    cross = total[kdim:]
    gt[...] = (total[:kdim] + (cross + cross.T)).reshape(gt.shape)
    gram.scatter()
    coefficients.wait()

    lane = lax.broadcasted_iota(jnp.int32, (1, 1, cz), 2)
    from_low = jnp.where(lane == 0, 0.0, 0.5)
    from_high = jnp.where(lane == cz - 1, 0.0, 0.5)
    step = 16
    groups = kdim // step // (cy // 2)

    def stencil_plane(x, before):
        diag = 9.0 + coef[x]

        def chunk(b, c):
            if before is not None:
                products(before, b)
            for part in range(groups):
                rows(b * groups + part)
            return c

        def rows(b):
            ks = pl.ds(pl.multiple_of(b * step, step), step)
            middle = s2[x + 1, :, ks, :]
            g = middle + 0.5 * (s2[x, :, ks, :] + s2[x + 2, :, ks, :])
            for y in range(cy):
                v = g[y]
                if y == 0:
                    v = v + 0.5 * g[1]
                elif y == cy - 1:
                    v = v + 0.5 * g[cy - 2]
                else:
                    v = v + 0.5 * (g[y - 1] + g[y + 1])
                v = (
                    v
                    + from_low[0] * pltpu.roll(v, 1, 1)
                    + from_high[0] * pltpu.roll(v, cz - 1, 1)
                )
                high, low = parts_of(diag[y : y + 1, :] * middle[y] - v)
                ab[x, ks, y * cz : (y + 1) * cz] = high
                ab[x, pl.ds(pl.multiple_of(kdim + b * step, step), step), y * cz : (y + 1) * cz] = low

        lax.fori_loop(0, cy // 2, chunk, 0)
        pltpu.make_async_copy(ab.at[x], applied.at[x], out_sem.at[x]).start()

    def products(x, b):
        at = pl.ds(pl.multiple_of(b * 2 * cz, 2 * cz), 2 * cz)
        hacc[...] += lax.dot_general(
            sb[x, :, at], ab[x, 0:kdim, at], NT, preferred_element_type=F32
        )
        hlow[...] += lax.dot_general(
            sb[x, 0:kdim, at], ab[x, kdim : 2 * kdim, at], NT, preferred_element_type=F32
        )

    def all_products(x):
        for b in range(cy // 2):
            products(x, b)

    def stencil_next(x, c):
        stencil_plane(x, x - 1)
        return c

    hacc[...] = jnp.zeros(hacc.shape, F32)
    hlow[...] = jnp.zeros(hlow.shape, F32)
    half = cx // 2
    stencil_plane(1, None)
    lax.fori_loop(2, half, stencil_next, 0)
    gram.spread()
    lax.fori_loop(half, cx - 1, stencil_next, 0)

    @pl.when(me > 0)
    def _():
        to_right.wait_recv()

    @pl.when(me == 0)
    def _():
        s2[0] = jnp.zeros(s2.shape[1:], F32)

    stencil_plane(0, cx - 2)

    @pl.when(me < n - 1)
    def _():
        to_left.wait_recv()

    @pl.when(me == n - 1)
    def _():
        s2[cx + 1] = jnp.zeros(s2.shape[1:], F32)

    stencil_plane(cx - 1, 0)
    all_products(cx - 1)
    ht[...] = (hacc[:kdim] + hacc[kdim:] + hlow[...]).reshape(ht.shape)
    hess.scatter()

    gram.finish()
    ncells = cx * n * cy * cz
    full = gtot[...].reshape(kdim, kdim) * (1.0 / ncells)
    rows, cols = (lax.broadcasted_iota(jnp.int32, (kdim, kdim), d) for d in (0, 1))
    on_diagonal = jnp.where(rows == cols, full, 0.0)
    norm = jnp.sqrt(jnp.sum(on_diagonal, axis=0, keepdims=True))
    inv_norm = 1.0 / norm
    rest = full * inv_norm * (1.0 / jnp.sqrt(jnp.sum(on_diagonal, axis=1, keepdims=True)))
    panels = kdim // 8
    done, rest = eliminate(rest, panels // 2, 0)
    hess.spread()
    more, rest = eliminate(rest, panels - panels // 2, panels // 2)
    rest = jnp.concatenate(done + more, axis=0)
    pivots = jnp.sum(jnp.where(rows == cols, rest, 0.0), axis=1, keepdims=True)
    packed[...] = rest * (1.0 / jnp.sqrt(pivots)) * jnp.where(cols >= rows, norm, inv_norm)
    hess.finish()
    hsum[...] = htot[...].reshape(kdim, kdim) * (1.0 / ncells)

    pl.when(me < n - 1)(to_right.wait_send)
    pl.when(me > 0)(to_left.wait_send)

    def written(x, c):
        pltpu.make_async_copy(ab.at[x], applied.at[x], out_sem.at[x]).wait()
        return c

    lax.fori_loop(0, cx, written, 0)


def image_kernel(packed, hsum, applied, factor, image, reduced, ab, buf, load_sem, out_sem):
    cx, cy, kdim, cz = buf.shape

    def load(x):
        return pltpu.make_async_copy(applied.at[x], ab.at[x], load_sem.at[x])

    def start(x, c):
        load(x).start()
        return c

    lax.fori_loop(0, cx, start, 0)
    a = packed[...]
    row = lax.broadcasted_iota(jnp.int32, (kdim, kdim), 0)
    col = lax.broadcasted_iota(jnp.int32, (kdim, kdim), 1)
    pivots = jnp.sum(jnp.where(row == col, a, 0.0), axis=1, keepdims=True)
    factor[...] = jnp.where(col >= row, a, 0.0)
    inverse = jnp.where(col < row, a, jnp.where(row == col, 1.0 / pivots, 0.0))
    high, low = parts_of(inverse)
    twice = jnp.concatenate([high, high], axis=1)

    def store(x, y):
        return pltpu.make_async_copy(
            buf.at[x, y], image.at[:, x * cy + y, 0, :], out_sem.at[x, y]
        )

    def plane(x, c):
        load(x).wait()
        for y in range(0, cy, 2):
            at = slice(y * cz, (y + 2) * cz)
            value = jnp.dot(twice, ab[x, :, at], preferred_element_type=F32) + jnp.dot(
                low, ab[x, 0:kdim, at], preferred_element_type=F32
            )
            buf[x, y] = value[:, :cz]
            buf[x, y + 1] = value[:, cz:]
            store(x, y).start()
            store(x, y + 1).start()
        return c

    lax.fori_loop(0, cx, plane, 0, unroll=2)
    left = jnp.dot(inverse, hsum[...], precision=HIGH, preferred_element_type=F32)
    reduced[...] = lax.dot_general(left, inverse, NT, precision=HIGH, preferred_element_type=F32)

    def finish(x, c):
        for y in range(cy):
            store(x, y).wait()
        return c

    lax.fori_loop(0, cx, finish, 0)


def shards(n, snapshots, coefficient):
    kdim, cx, cy, cz = snapshots.shape
    owners = min(n, kdim // 8)
    rows = kdim // owners
    vmem = pl.BlockSpec(memory_space=pltpu.VMEM)
    hbm = pl.BlockSpec(memory_space=pl.ANY)
    square = jax.ShapeDtypeStruct((kdim, kdim), F32)
    dma = pltpu.SemaphoreType.DMA
    summed = [
        pltpu.VMEM((owners, rows, kdim), F32),
        pltpu.VMEM((n, rows, kdim), F32),
        pltpu.VMEM((owners, rows, kdim), F32),
    ]
    sum_sems = [dma((n,)), dma((n,)), dma((n,)), dma((owners,))]
    packed, hsum, applied = pl.pallas_call(
        functools.partial(reduce_kernel, n, owners),
        out_shape=(square, square, jax.ShapeDtypeStruct((cx, 2 * kdim, cy * cz), BF16)),
        in_specs=[hbm, hbm],
        out_specs=(vmem, vmem, hbm),
        scratch_shapes=[
            pltpu.VMEM((cx, cy, cz), F32),
            dma,
            pltpu.VMEM((cx + 2, cy, kdim, cz), F32),
            pltpu.VMEM((cx, 2 * kdim, cy * cz), BF16),
            pltpu.VMEM((cx, 2 * kdim, cy * cz), BF16),
            pltpu.VMEM((2 * kdim, kdim), F32),
            pltpu.VMEM((kdim, kdim), F32),
            *summed,
            *summed,
            dma((cx, cy)), dma((2,)), dma((2,)), dma((cx,)),
            *sum_sems,
            *sum_sems,
        ],
        compiler_params=pltpu.CompilerParams(
            collective_id=0, has_side_effects=True, vmem_limit_bytes=VMEM_BYTES
        ),
        name="reduce_kernel",
    )(snapshots.reshape(kdim, cx * cy, 1, cz), coefficient)
    factor, image, reduced = pl.pallas_call(
        image_kernel,
        out_shape=(square, jax.ShapeDtypeStruct((kdim, cx * cy, 1, cz), F32), square),
        in_specs=[vmem, vmem, hbm],
        out_specs=(vmem, hbm, vmem),
        scratch_shapes=[
            pltpu.VMEM((cx, 2 * kdim, cy * cz), BF16),
            pltpu.VMEM((cx, cy, kdim, cz), F32),
            dma((cx,)), dma((cx, cy)),
        ],
        compiler_params=pltpu.CompilerParams(vmem_limit_bytes=VMEM_BYTES),
        name="image_kernel",
    )(packed, hsum, applied)
    return factor, image.reshape(kdim, cx, cy, cz), reduced


def solution(mesh):
    placed = (P("groups", "gx", None, None), P(("groups", "gx"), None, None))
    return jax.shard_map(
        functools.partial(shards, mesh.shape["gx"]),
        mesh=mesh,
        in_specs=placed,
        out_specs=(P("groups", None), P(None, ("groups", "gx"), None, None), P("groups", None)),
        check_vma=False,
    )
```
